32 devices in a mesh: dp: 8 (over z, y), seq: 4 (over x, core).
Axes of the slice: x: 2, y: 2, z: 4, core: 2. Of those that a mesh axis runs over, the one named last changes fastest.
Arguments:
- spatial_input_tokens: bfloat16 [16, 4, 64, 1152], P('dp', 'seq'), may hold values from -6 to 6
- upstream: bfloat16 [16, 4, 64, 1152], P('dp', None, 'seq'), may hold values from -6 to 6
- modulation: float32 [16, 6, 1152], P('dp'), may hold values from -3 to 3
- spatial_query_key_value: bfloat16 [3, 1152, 576], P(None, 'seq'), may hold values from -0.1875 to 0.1875
- spatial_output_weight: bfloat16 [576, 1152], P('seq'), may hold values from -0.25 to 0.25
- temporal_query_key_value: bfloat16 [3, 1152, 576], P(None, 'seq'), may hold values from -0.1875 to 0.1875
- temporal_output_weight: bfloat16 [576, 1152], P('seq'), may hold values from -0.25 to 0.25
- adapter_down_maps: float32 [2, 2, 32, 1152], replicated, may hold values from -0.1875 to 0.1875
- adapter_up_maps: float32 [2, 2, 32, 576], replicated, may hold values from -1 to 1
Outputs:
- grad_frames: bfloat16 [16, 4, 64, 1152], P('dp', 'seq')
- grad_down: float32 [2, 2, 32, 1152], replicated
- grad_up: float32 [2, 2, 32, 576], replicated
The draws below stay inside these ranges and needn't reach their ends.
All inputs are finite; a program needn't handle non-finite values.
Results may differ from the reference program's by a relative error of at most 0.015.
Values may be sent and summed in bfloat16 or wider, within the bound.
A program may use at most 128 MiB of HBM per device.

```python
import jax
import jax.numpy as jnp
from jax import lax

MODEL_WIDTH = 1152
LOCAL_HEADS = 8
HEAD_WIDTH = 72
ADAPTER_RANK = 32
S = 64
F = 4
BATCH = 16


def block_levels(key, extent, cuts, low, high):
    factor_of = 1.0
    for axis_at, parts in cuts:
        draws = jax.random.uniform(jax.random.fold_in(jax.random.fold_in(key, 6), axis_at), (parts,), jnp.float32, low / len(cuts), high / len(cuts))
        factor_of = factor_of * jnp.repeat(jnp.exp(draws), extent[axis_at] // parts).reshape((-1,) + (1,) * (len(extent) - 1 - axis_at))
    return factor_of


def centred(rng, dims, deviation, most, cuts=(), held_as=jnp.bfloat16):
    gain = block_levels(rng, dims, cuts, -0.22, 0.18) if cuts else 1.0
    array = jax.random.normal(rng, dims, jnp.float32) * deviation * gain
    return jnp.minimum(jnp.maximum(array, -most), most).astype(held_as)


def setup_inputs(seed: int = 0) -> dict:
    key_of = jax.random.split(jax.random.key(seed), 10)
    spatial_input_tokens = centred(key_of[0], (BATCH, F, S, MODEL_WIDTH), 1.0, 6.0, ((0, 8), (1, 4)))
    upstream = centred(key_of[1], (BATCH, F, S, MODEL_WIDTH), 1.0, 6.0, ((0, 8), (2, 4)))
    modulation = centred(key_of[2], (BATCH, 6, MODEL_WIDTH), 0.5, 3.0, ((0, 8),), jnp.float32)
    spatial_query_key_value = centred(key_of[3], (3, MODEL_WIDTH, LOCAL_HEADS * HEAD_WIDTH), MODEL_WIDTH ** -0.5, 0.1875, ((1, 4),))
    spatial_output_weight = centred(key_of[4], (LOCAL_HEADS * HEAD_WIDTH, MODEL_WIDTH), (LOCAL_HEADS * HEAD_WIDTH) ** -0.5, 0.25, ((0, 4),))
    temporal_query_key_value = centred(key_of[5], (3, MODEL_WIDTH, LOCAL_HEADS * HEAD_WIDTH), MODEL_WIDTH ** -0.5, 0.1875, ((1, 4),))
    temporal_output_weight = centred(key_of[6], (LOCAL_HEADS * HEAD_WIDTH, MODEL_WIDTH), (LOCAL_HEADS * HEAD_WIDTH) ** -0.5, 0.25, ((0, 4),))
    adapter_down_maps = centred(key_of[7], (2, 2, ADAPTER_RANK, MODEL_WIDTH), MODEL_WIDTH ** -0.5, 0.1875, (), jnp.float32)
    adapter_up_maps = centred(key_of[8], (2, 2, ADAPTER_RANK, LOCAL_HEADS * HEAD_WIDTH), ADAPTER_RANK ** -0.5, 1.0, (), jnp.float32)
    return {"spatial_input_tokens": spatial_input_tokens, "upstream": upstream, "modulation": modulation, "spatial_query_key_value": spatial_query_key_value, "spatial_output_weight": spatial_output_weight, "temporal_query_key_value": temporal_query_key_value, "temporal_output_weight": temporal_output_weight, "adapter_down_maps": adapter_down_maps, "adapter_up_maps": adapter_up_maps}


EPSILON = 1e-06
full_precision = lax.Precision.HIGHEST

def head_norm(vectors):
    return (vectors * lax.rsqrt(lax.optimization_barrier(jnp.mean(vectors * vectors, axis=-1, keepdims=True)) + EPSILON)).astype(jnp.bfloat16)

def attend(normed_query, normed_keys, values, temporal):
    factor = normed_query.shape[-1] ** (-0.5)
    query32 = normed_query.astype(jnp.float32)
    keys32 = normed_keys.astype(jnp.float32)
    values32 = values.astype(jnp.float32)
    if temporal:
        scores = jnp.einsum('bfshd,bgshd->bshfg', query32, keys32)
    else:
        scores = jnp.einsum('bfshd,bfthd->bfhst', query32, keys32)
    weights = jnp.exp(scores * factor)
    probabilities = (weights / lax.optimization_barrier(jnp.sum(weights, axis=-1, keepdims=True))).astype(jnp.bfloat16).astype(jnp.float32)
    if temporal:
        attended = jnp.einsum('bshfg,bgshd->bfshd', probabilities, values32)
    else:
        attended = jnp.einsum('bfhst,bfthd->bfshd', probabilities, values32)
    return attended.astype(jnp.bfloat16)

def block(stream, modrows, proj_in, proj_out, down_maps, up_maps, temporal):
    features = stream.shape[-1]
    leading = stream.shape[:3]
    values32 = stream.astype(jnp.float32)
    center = values32 - lax.optimization_barrier(jnp.mean(values32, axis=-1, keepdims=True))
    normed = center * lax.rsqrt(lax.optimization_barrier(jnp.mean(center * center, axis=-1, keepdims=True)) + EPSILON)
    shift_rows = modrows[:, 0][:, None, None, :]
    scale_rows = modrows[:, 1][:, None, None, :]
    gate_rows = modrows[:, 2][:, None, None, :]
    inputs = (normed * (1.0 + scale_rows) + shift_rows).astype(jnp.bfloat16)
    token_rows = inputs.reshape(-1, features)
    rows_wide = token_rows.astype(jnp.float32)
    low_query = jnp.dot(rows_wide, down_maps[0].T, precision=full_precision).astype(jnp.bfloat16)
    low_value = jnp.dot(rows_wide, down_maps[1].T, precision=full_precision).astype(jnp.bfloat16)
    query = jnp.dot(token_rows, proj_in[0], preferred_element_type=jnp.float32) + jnp.dot(low_query.astype(jnp.float32), up_maps[0], precision=full_precision)
    key_vectors = jnp.dot(token_rows, proj_in[1], preferred_element_type=jnp.float32)
    values = (jnp.dot(token_rows, proj_in[2], preferred_element_type=jnp.float32) + jnp.dot(low_value.astype(jnp.float32), up_maps[1], precision=full_precision)).astype(jnp.bfloat16)
    inner_width = query.shape[-1]
    head_shape = (leading[0], leading[1], leading[2], LOCAL_HEADS, inner_width // LOCAL_HEADS)
    attended = attend(head_norm(query.reshape(head_shape)), head_norm(key_vectors.reshape(head_shape)), values.reshape(head_shape), temporal)
    projected = jnp.dot(attended.reshape(-1, inner_width), proj_out, preferred_element_type=jnp.float32)
    return values32 + gate_rows * projected.reshape(leading[0], leading[1], leading[2], features)

def reference(spatial_input_tokens, upstream, modulation, spatial_query_key_value, spatial_output_weight, temporal_query_key_value, temporal_output_weight, adapter_down_maps, adapter_up_maps):

    def one_sample(carry, inputs):
        sample_index, cotangent, modrows = inputs

        def forward_pass(stream, down_all, up_all):
            hidden = block(stream[None], modrows[None, 0:3], spatial_query_key_value, spatial_output_weight, down_all[0], up_all[0], False).astype(jnp.bfloat16)
            return block(hidden, modrows[None, 3:6], temporal_query_key_value, temporal_output_weight, down_all[1], up_all[1], True)
        layer_output, vector_jacobian = jax.vjp(forward_pass, sample_index, adapter_down_maps, adapter_up_maps)
        grad_in, part_down, part_up = vector_jacobian(cotangent[None].astype(layer_output.dtype))
        return ((carry[0] + part_down, carry[1] + part_up), grad_in)
    start_row = (jnp.zeros_like(adapter_down_maps), jnp.zeros_like(adapter_up_maps))
    sums, grad_frames = lax.scan(one_sample, start_row, (spatial_input_tokens, upstream, modulation))
    factor = float(BATCH * F * S) ** (-0.5)
    return (grad_frames, sums[0] * factor, sums[1] * factor)
```

```python
import functools

import jax
import jax.numpy as jnp
from jax import lax
from jax.experimental import pallas as pl
from jax.experimental.pallas import tpu as pltpu
from jax.sharding import PartitionSpec as P

LOCAL_HEADS = 8
EPSILON = 1e-06
MESH = pl.DeviceIdType.MESH
BF, F32 = jnp.bfloat16, jnp.float32
VMEM = pl.BlockSpec(memory_space=pltpu.VMEM)
ANY = pl.BlockSpec(memory_space=pl.ANY)
VMEM_BYTES = 56 * 2**20


def nn(a, b):
    return lax.dot_general(a, b, (((1,), (0,)), ((), ())), preferred_element_type=F32)


def nt(a, b):
    return lax.dot_general(a, b, (((1,), (1,)), ((), ())), preferred_element_type=F32)


def tn(a, b):
    return lax.dot_general(a, b, (((0,), (0,)), ((), ())), preferred_element_type=F32)


def nt_full(a, b):
    return lax.dot_general(
        a, b, (((1,), (1,)), ((), ())), preferred_element_type=F32, precision=lax.Precision.HIGHEST
    )


def nn_full(a, b):
    return lax.dot_general(
        a, b, (((1,), (0,)), ((), ())), preferred_element_type=F32, precision=lax.Precision.HIGHEST
    )


class Layer:
    def __init__(self, z, mod_ref, row, down_ref, up_ref, layer, group_mask):
        self.tokens, self.width = z.shape
        self.batch = mod_ref.shape[0]
        self.mod_ref, self.row = mod_ref, row
        self.z = z.astype(F32)
        center = self.z - jnp.mean(self.z, axis=-1, keepdims=True)
        self.rstd = lax.rsqrt(jnp.mean(center * center, axis=-1, keepdims=True) + EPSILON)
        self.normed = center * self.rstd
        self.u = (self.normed * (1.0 + self.rows(1)) + self.rows(0)).astype(BF)
        rank = down_ref.shape[2]
        inner = up_ref.shape[3]
        self.rank, self.inner = rank, inner
        self.down = down_ref[layer].reshape(2 * rank, self.width).astype(BF)
        zero = jnp.zeros((rank, inner), BF)
        self.up_q = jnp.concatenate([up_ref[layer, 0].astype(BF), zero], axis=0)
        self.up_v = jnp.concatenate([zero, up_ref[layer, 1].astype(BF)], axis=0)
        self.head = inner // LOCAL_HEADS
        lane_head = lax.broadcasted_iota(jnp.int32, (1, inner), 1) // self.head
        self.head_rows = [(lane_head == h).astype(F32).astype(BF) for h in range(LOCAL_HEADS)]
        self.head_rows32 = [(lane_head == h).astype(F32) for h in range(LOCAL_HEADS)]
        spread_head = lax.broadcasted_iota(jnp.int32, (128, inner), 1) // self.head
        spread_row = lax.broadcasted_iota(jnp.int32, (128, inner), 0)
        self.spread = (spread_head == spread_row).astype(F32)
        self.group_mask = group_mask

    def rows(self, j):
        span = self.tokens // self.batch
        return jnp.concatenate(
            [
                jnp.broadcast_to(self.mod_ref[b, self.row + j][None, :], (span, self.width))
                for b in range(self.batch)
            ],
            axis=0,
        )

    def per_head(self, values):
        return nt_full(values, self.spread) * (1.0 / self.head)

    def to_lanes(self, values):
        return nn_full(values, self.spread)

    def big(self, values):
        return jnp.concatenate([values * m for m in self.head_rows], axis=0)

    def fold(self, values):
        t = self.tokens
        return sum(
            values[h * t : (h + 1) * t] * self.head_rows32[h] for h in range(LOCAL_HEADS)
        )

    def project(self, w_q, w_k, w_v):
        self.low = nt(self.u, self.down).astype(BF)
        self.q = nn(self.u, w_q[...]) + nn(self.low, self.up_q)
        self.k = nn(self.u, w_k[...])
        self.v = (nn(self.u, w_v[...]) + nn(self.low, self.up_v)).astype(BF)

    def attend(self):
        t = self.tokens
        self.r_q = self.to_lanes(lax.rsqrt(self.per_head(self.q * self.q) + EPSILON))
        self.r_k = self.to_lanes(lax.rsqrt(self.per_head(self.k * self.k) + EPSILON))
        self.qn = (self.q * self.r_q).astype(BF)
        self.kn_big = self.big((self.k * self.r_k).astype(BF))
        self.v_big = self.big(self.v)
        scores = nt(self.qn, self.kn_big)
        factor = self.head ** (-0.5)
        probs = []
        for h in range(LOCAL_HEADS):
            e = jnp.where(self.group_mask, jnp.exp(scores[:, h * t : (h + 1) * t] * factor), 0.0)
            probs.append(e / jnp.sum(e, axis=-1, keepdims=True))
        self.probs32 = probs
        self.probs = jnp.concatenate([p.astype(BF) for p in probs], axis=1)

    def output(self, w_o):
        att = nn(self.probs, self.v_big).astype(BF)
        return self.z + self.rows(2) * nn(att, w_o[...])

    def backward(self, dout, w_q, w_k, w_v, w_o):
        t = self.tokens
        datt = nt((self.rows(2) * dout).astype(BF), w_o[...]).astype(BF)
        dprobs = nt(datt, self.v_big)
        dv = self.fold(tn(self.probs, datt)).astype(BF)
        factor = self.head ** (-0.5)
        ds = []
        for h in range(LOCAL_HEADS):
            dp = dprobs[:, h * t : (h + 1) * t].astype(BF).astype(F32)
            p = self.probs32[h]
            ds.append((p * (dp - jnp.sum(p * dp, axis=-1, keepdims=True)) * factor).astype(BF))
        ds = jnp.concatenate(ds, axis=1)
        dqn = nn(ds, self.kn_big).astype(BF).astype(F32)
        dkn = self.fold(tn(ds, self.qn)).astype(BF).astype(F32)

        def norm_back(d, x, r):
            xn = x * r
            return r * (d - xn * self.to_lanes(self.per_head(d * xn)))

        dq = norm_back(dqn, self.q, self.r_q).astype(BF)
        dk = norm_back(dkn, self.k, self.r_k).astype(BF)
        dlow = (nt(dq, self.up_q) + nt(dv, self.up_v)).astype(BF)
        du = nt(dq, w_q[...]) + nt(dk, w_k[...]) + nt(dv, w_v[...]) + nn(dlow, self.down)
        du = du.astype(BF).astype(F32)
        grad_down = tn(dlow, self.u)
        grad_up = jnp.concatenate(
            [tn(self.low, dq)[: self.rank], tn(self.low, dv)[self.rank :]], axis=0
        )
        dn = du * (1.0 + self.rows(1))
        dz = dout + self.rstd * (
            dn
            - jnp.mean(dn, axis=-1, keepdims=True)
            - self.normed * jnp.mean(dn * self.normed, axis=-1, keepdims=True)
        )
        return dz, grad_down, grad_up


def spatial_mask(tokens, positions):
    row = lax.broadcasted_iota(jnp.int32, (tokens, tokens), 0)
    col = lax.broadcasted_iota(jnp.int32, (tokens, tokens), 1)
    return row // positions == col // positions


def temporal_mask(tokens, batch, positions):
    row = lax.broadcasted_iota(jnp.int32, (tokens, tokens), 0)
    col = lax.broadcasted_iota(jnp.int32, (tokens, tokens), 1)
    span = tokens // batch
    return (row // span == col // span) & (row % positions == col % positions)


def spatial_forward_kernel(positions, z, mod, down, up, w_in, w_out, hidden, q, k, v, low):
    layer = Layer(z[...], mod, 0, down, up, 0, spatial_mask(z.shape[0], positions))
    layer.project(w_in.at[0], w_in.at[1], w_in.at[2])
    layer.attend()
    hidden[...] = layer.output(w_out).astype(BF)
    q[...], k[...], v[...], low[...] = layer.q, layer.k, layer.v, layer.low


def temporal_kernel(positions, z, upstream, mod, down, up, w_in, w_out, dz, g_down, g_up):
    layer = Layer(
        z[...], mod, 3, down, up, 1, temporal_mask(z.shape[0], mod.shape[0], positions)
    )
    layer.project(w_in.at[0], w_in.at[1], w_in.at[2])
    layer.attend()
    grad, g_down[...], g_up[...] = layer.backward(
        upstream[...].astype(F32), w_in.at[0], w_in.at[1], w_in.at[2], w_out
    )
    dz[...] = grad.astype(BF)


def spatial_backward_kernel(
    positions, z, cotangent, q, k, v, low, mod, down, up, w_in, w_out, dz, g_down, g_up
):
    layer = Layer(z[...], mod, 0, down, up, 0, spatial_mask(z.shape[0], positions))
    layer.q, layer.k, layer.v, layer.low = q[...], k[...], v[...], low[...]
    layer.attend()
    grad, g_down[...], g_up[...] = layer.backward(
        cotangent[...].astype(F32), w_in.at[0], w_in.at[1], w_in.at[2], w_out
    )
    dz[...] = grad.astype(BF)


def vmem_call(kernel, out_shape, *operands):
    return pl.pallas_call(
        kernel,
        out_shape=out_shape,
        in_specs=[VMEM] * len(operands),
        out_specs=[VMEM] * len(out_shape),
        compiler_params=pltpu.CompilerParams(vmem_limit_bytes=VMEM_BYTES),
    )(*operands)


def gather_kernel(
    n_dp, n_seq, in_s, out_s, in_t, out_t, all_in_s, all_out_s, all_in_t, all_out_t, own_sem,
    sib_send, sib_recv, x_send, x_recv, y_send, y_recv, fwd_send, fwd_recv,
):
    d, s = lax.axis_index("dp"), lax.axis_index("seq")
    chips = n_seq // 2
    chip, core = s // 2, s % 2
    other_core = 2 * chip + 1 - core
    pair = d + 1 - 2 * (d % 2)

    def at(chip_index):
        return 2 * lax.rem(chip_index + chips, chips)

    barrier = pltpu.get_barrier_semaphore()
    greet = [(d, other_core), (pair, s)] + [(d, at(chip + j) + core) for j in range(1, chips)]
    for target in greet:
        pl.semaphore_signal(barrier, inc=1, device_id=target, device_id_type=MESH)
    pl.semaphore_wait(barrier, len(greet))

    def source(piece):
        mine, out = (in_s, out_s) if piece < 4 else (in_t, out_t)
        return mine.at[piece % 4] if piece % 4 < 3 else out

    def place(piece, shard):
        full, out = (all_in_s, all_out_s) if piece < 4 else (all_in_t, all_out_t)
        return full.at[piece % 4, shard] if piece % 4 < 3 else out.at[shard]

    def remote(src, dst, send, recv, target):
        return pltpu.make_async_remote_copy(
            src_ref=src, dst_ref=dst, send_sem=send, recv_sem=recv,
            device_id=target, device_id_type=MESH,
        )

    def own(piece):
        return pltpu.make_async_copy(source(piece), place(piece, s), own_sem.at[piece])

    def to_sibling(piece):
        return remote(
            source(piece), place(piece, s), sib_send.at[piece], sib_recv.at[piece], (d, other_core)
        )

    def across(j, piece):
        return remote(
            source(piece), place(piece, s), x_send.at[j - 1, piece], x_recv.at[j - 1, piece],
            (d, at(chip + j) + core),
        )

    def relay(j, piece, sems, target):
        held = place(piece, at(chip - j) + core)
        return remote(held, held, sems[0].at[j - 1, piece], sems[1].at[j - 1, piece], target)

    def to_pair(j, piece):
        return relay(j, piece, (y_send, y_recv), (pair, s))

    def to_core(j, piece):
        return relay(j, piece, (fwd_send, fwd_recv), (d, other_core))

    def run(half):
        layers = [0, 4]
        first = [[base + 2 * half, base + 2 * half + 1] for base in layers]
        second = [[base + 2 - 2 * half, base + 3 - 2 * half] for base in layers]
        for layer in range(2):
            for piece in first[layer]:
                for j in range(1, chips):
                    across(j, piece).start()
        for piece in range(8):
            to_sibling(piece).start()
            own(piece).start()
        for layer in range(2):
            for piece in first[layer]:
                for j in range(1, chips):
                    across(j, piece).wait_recv()
                    to_pair(j, piece).start()
                    to_core(j, piece).start()
            for piece in second[layer]:
                for j in range(1, chips):
                    to_pair(j, piece).wait_recv()
                    to_core(j, piece).start()
        for piece in range(8):
            to_sibling(piece).wait()
            own(piece).wait()
            for j in range(1, chips):
                to_core(j, piece).wait()
        for layer in range(2):
            for piece in first[layer]:
                for j in range(1, chips):
                    across(j, piece).wait_send()
                    to_pair(j, piece).wait_send()

    for half in range(2):
        pl.when(d % 2 == half)(functools.partial(run, half))


def gather_weights(n_dp, n_seq, weights):
    in_s, out_s, in_t, out_t = weights
    links = max(n_seq // 2 - 1, 1)
    dma = pltpu.SemaphoreType.DMA
    shapes = []
    for w in weights:
        full = w.shape[:-2] + (n_seq,) + w.shape[-2:]
        shapes.append(jax.ShapeDtypeStruct(full, BF))
    gathered = pl.pallas_call(
        functools.partial(gather_kernel, n_dp, n_seq),
        out_shape=shapes,
        in_specs=[ANY] * 4,
        out_specs=[ANY] * 4,
        scratch_shapes=[dma((8,))] * 3 + [dma((links, 8))] * 6,
        compiler_params=pltpu.CompilerParams(collective_id=0, has_side_effects=True),
    )(*weights)
    return [
        g.reshape(g.shape[:-3] + (g.shape[-3] * g.shape[-2], g.shape[-1])) for g in gathered
    ]


def sum_kernel(
    n_dp, n_seq, x, out, wide, got_seq, part, got_dp, full, s1, r1, s2, r2, s3, r3, s4, r4
):
    d, s = lax.axis_index("dp"), lax.axis_index("seq")

    def seq_at(j):
        return lax.rem(s + j, n_seq)

    def dp_at(j):
        return lax.rem(d + j, n_dp)

    barrier = pltpu.get_barrier_semaphore()
    for j in range(1, n_seq):
        pl.semaphore_signal(barrier, inc=1, device_id=(d, seq_at(j)), device_id_type=MESH)
    for j in range(1, n_dp):
        pl.semaphore_signal(barrier, inc=1, device_id=(dp_at(j), s), device_id_type=MESH)
    wide[...] = x[...].astype(BF)
    pl.semaphore_wait(barrier, n_seq - 1 + n_dp - 1)

    def exchange(count, source, dest, send, recv, target):
        copies = [
            pltpu.make_async_remote_copy(
                src_ref=source(j), dst_ref=dest(j), send_sem=send.at[j - 1],
                recv_sem=recv.at[j - 1], device_id=target(j), device_id_type=MESH,
            )
            for j in range(1, count)
        ]
        for copy in copies:
            copy.start()
        return copies

    to_seq = lambda j: (d, seq_at(j))
    to_dp = lambda j: (dp_at(j), s)
    pending = exchange(
        n_seq, lambda j: wide.at[seq_at(j)], lambda j: got_seq.at[j - 1], s1, r1, to_seq
    )
    for copy in pending:
        copy.wait_recv()
    total = x[s]
    for j in range(1, n_seq):
        total = total + got_seq[j - 1].astype(F32)
    part[...] = total.astype(BF)
    more = exchange(n_dp, lambda j: part.at[dp_at(j)], lambda j: got_dp.at[j - 1], s2, r2, to_dp)
    for copy in more:
        copy.wait_recv()
    mine = part[d].astype(F32)
    for j in range(1, n_dp):
        mine = mine + got_dp[j - 1].astype(F32)
    full[s, d] = mine.astype(BF)
    pending += more
    more = exchange(n_dp, lambda j: full.at[s, d], lambda j: full.at[s, d], s3, r3, to_dp)
    for copy in more:
        copy.wait_recv()
    pending += more
    more = exchange(n_seq, lambda j: full.at[s], lambda j: full.at[s], s4, r4, to_seq)
    for copy in more:
        copy.wait_recv()
    out[...] = full[...].astype(F32)
    for copy in pending + more:
        copy.wait_send()


def sum_everywhere(n_dp, n_seq, flat):
    total = flat.shape[0]
    unit = 16 * 128
    devices = n_dp * n_seq
    rows = -(-total // (devices * unit)) * 16
    padded = jnp.pad(flat, (0, devices * rows * 128 - total))
    shape = (n_seq, n_dp, rows, 128)
    dma = pltpu.SemaphoreType.DMA
    seq_sem, dp_sem = dma((n_seq - 1,)), dma((n_dp - 1,))
    summed = pl.pallas_call(
        functools.partial(sum_kernel, n_dp, n_seq),
        out_shape=jax.ShapeDtypeStruct(shape, F32),
        in_specs=[VMEM],
        out_specs=VMEM,
        scratch_shapes=[
            pltpu.VMEM(shape, BF),
            pltpu.VMEM((n_seq - 1,) + shape[1:], BF),
            pltpu.VMEM(shape[1:], BF),
            pltpu.VMEM((n_dp - 1,) + shape[2:], BF),
            pltpu.VMEM(shape, BF),
            seq_sem, seq_sem, dp_sem, dp_sem, dp_sem, dp_sem, seq_sem, seq_sem,
        ],
        compiler_params=pltpu.CompilerParams(
            collective_id=1, has_side_effects=True, vmem_limit_bytes=VMEM_BYTES
        ),
    )(padded.reshape(shape))
    return summed.reshape(-1)[:total]


def per_device(n_dp, n_seq, z, upstream, mod, in_s, out_s, in_t, out_t, down, up):
    w_in_s, w_out_s, w_in_t, w_out_t = gather_weights(n_dp, n_seq, (in_s, out_s, in_t, out_t))
    batch, frames_here, positions, width = z.shape
    frames = frames_here * n_seq
    positions_here = positions // n_seq
    inner, rank = up.shape[3], up.shape[2]
    tokens = batch * frames_here * positions
    factor = float(batch * n_dp * frames * positions) ** (-0.5)
    shape = jax.ShapeDtypeStruct
    z_rows = z.reshape(tokens, width)
    hidden, q, k, v, low = vmem_call(
        functools.partial(spatial_forward_kernel, positions),
        [
            shape((tokens, width), BF), shape((tokens, inner), F32), shape((tokens, inner), F32),
            shape((tokens, inner), BF), shape((tokens, 2 * rank), BF),
        ],
        z_rows, mod, down, up, w_in_s, w_out_s,
    )
    by_position = lax.all_to_all(
        hidden.reshape(z.shape), "seq", split_axis=2, concat_axis=1, tiled=True
    )
    grads = [
        shape((tokens, width), BF), shape((2 * rank, width), F32), shape((2 * rank, inner), F32)
    ]
    back, down_t, up_t = vmem_call(
        functools.partial(temporal_kernel, positions_here), grads,
        by_position.reshape(tokens, width), upstream.reshape(tokens, width), mod, down, up,
        w_in_t, w_out_t,
    )
    by_frame = lax.all_to_all(
        back.reshape(batch, frames, positions_here, width), "seq", split_axis=1, concat_axis=2,
        tiled=True,
    )
    grad, down_s, up_s = vmem_call(
        functools.partial(spatial_backward_kernel, positions), grads,
        z_rows, by_frame.reshape(tokens, width), q, k, v, low, mod, down, up, w_in_s, w_out_s,
    )
    flat = jnp.concatenate([a.reshape(-1) for a in (down_s, down_t, up_s, up_t)]) * factor
    flat = sum_everywhere(n_dp, n_seq, flat)
    cut = down.size
    return grad.reshape(z.shape), flat[:cut].reshape(down.shape), flat[cut:].reshape(up.shape)


def solution(mesh):
    placed = (
        P("dp", "seq", None, None),
        P("dp", None, "seq", None),
        P("dp", None, None),
        P(None, "seq", None),
        P("seq", None),
        P(None, "seq", None),
        P("seq", None),
        P(),
        P(),
    )
    return jax.shard_map(
        functools.partial(per_device, mesh.shape["dp"], mesh.shape["seq"]),
        mesh=mesh,
        in_specs=placed,
        out_specs=(P("dp", "seq", None, None), P(), P()),
        check_vma=False,
    )
```

```python
import functools

import jax
import jax.numpy as jnp
from jax import lax
from jax.experimental import pallas as pl
from jax.experimental.pallas import tpu as pltpu
from jax.sharding import PartitionSpec as P

LOCAL_HEADS = 8
EPSILON = 1e-06
MESH = pl.DeviceIdType.MESH
BF, F32 = jnp.bfloat16, jnp.float32
VMEM = pl.BlockSpec(memory_space=pltpu.VMEM)
ANY = pl.BlockSpec(memory_space=pl.ANY)
VMEM_BYTES = 56 * 2**20


def nn(a, b):
    return lax.dot_general(a, b, (((1,), (0,)), ((), ())), preferred_element_type=F32)


def nt(a, b):
    return lax.dot_general(a, b, (((1,), (1,)), ((), ())), preferred_element_type=F32)


def tn(a, b):
    return lax.dot_general(a, b, (((0,), (0,)), ((), ())), preferred_element_type=F32)


def nt_full(a, b):
    return lax.dot_general(
        a, b, (((1,), (1,)), ((), ())), preferred_element_type=F32, precision=lax.Precision.HIGHEST
    )


def nn_full(a, b):
    return lax.dot_general(
        a, b, (((1,), (0,)), ((), ())), preferred_element_type=F32, precision=lax.Precision.HIGHEST
    )


class Layer:
    def __init__(self, z, mod_ref, row, down_ref, up_ref, layer, group_mask):
        self.tokens, self.width = z.shape
        self.batch = mod_ref.shape[0]
        self.mod_ref, self.row = mod_ref, row
        self.z = z.astype(F32)
        center = self.z - jnp.mean(self.z, axis=-1, keepdims=True)
        self.rstd = lax.rsqrt(jnp.mean(center * center, axis=-1, keepdims=True) + EPSILON)
        self.normed = center * self.rstd
        self.u = (self.normed * (1.0 + self.rows(1)) + self.rows(0)).astype(BF)
        rank = down_ref.shape[2]
        inner = up_ref.shape[3]
        self.rank, self.inner = rank, inner
        self.down = down_ref[layer].reshape(2 * rank, self.width).astype(BF)
        zero = jnp.zeros((rank, inner), BF)
        self.up_q = jnp.concatenate([up_ref[layer, 0].astype(BF), zero], axis=0)
        self.up_v = jnp.concatenate([zero, up_ref[layer, 1].astype(BF)], axis=0)
        self.head = inner // LOCAL_HEADS
        lane_head = lax.broadcasted_iota(jnp.int32, (1, inner), 1) // self.head
        self.head_rows = [(lane_head == h).astype(F32).astype(BF) for h in range(LOCAL_HEADS)]
        self.head_rows32 = [(lane_head == h).astype(F32) for h in range(LOCAL_HEADS)]
        spread_head = lax.broadcasted_iota(jnp.int32, (128, inner), 1) // self.head
        spread_row = lax.broadcasted_iota(jnp.int32, (128, inner), 0)
        self.spread = (spread_head == spread_row).astype(F32)
        self.group_mask = group_mask

    def rows(self, j):
        span = self.tokens // self.batch
        return jnp.concatenate(
            [
                jnp.broadcast_to(self.mod_ref[b, self.row + j][None, :], (span, self.width))
                for b in range(self.batch)
            ],
            axis=0,
        )

    def per_head(self, values):
        return nt_full(values, self.spread) * (1.0 / self.head)

    def to_lanes(self, values):
        return nn_full(values, self.spread)

    def big(self, values):
        return jnp.concatenate([values * m for m in self.head_rows], axis=0)

    def fold(self, values):
        t = self.tokens
        return sum(
            values[h * t : (h + 1) * t] * self.head_rows32[h] for h in range(LOCAL_HEADS)
        )

    def project(self, w_q, w_k, w_v):
        self.low = nt(self.u, self.down).astype(BF)
        self.q = nn(self.u, w_q()) + nn(self.low, self.up_q)
        self.k = nn(self.u, w_k())
        self.v = (nn(self.u, w_v()) + nn(self.low, self.up_v)).astype(BF)

    def attend(self):
        t = self.tokens
        self.r_q = self.to_lanes(lax.rsqrt(self.per_head(self.q * self.q) + EPSILON))
        self.r_k = self.to_lanes(lax.rsqrt(self.per_head(self.k * self.k) + EPSILON))
        self.qn = (self.q * self.r_q).astype(BF)
        self.kn_big = self.big((self.k * self.r_k).astype(BF))
        self.v_big = self.big(self.v)
        scores = nt(self.qn, self.kn_big)
        factor = self.head ** (-0.5)
        probs = []
        for h in range(LOCAL_HEADS):
            e = jnp.where(self.group_mask, jnp.exp(scores[:, h * t : (h + 1) * t] * factor), 0.0)
            probs.append(e / jnp.sum(e, axis=-1, keepdims=True))
        self.probs32 = probs
        self.probs = jnp.concatenate([p.astype(BF) for p in probs], axis=1)

    def output(self, w_o):
        att = nn(self.probs, self.v_big).astype(BF)
        left, right = w_o()
        projected = jnp.concatenate([nn(att, left), nn(att, right)], axis=1)
        return self.z + self.rows(2) * projected

    def backward(self, dout, w_q, w_k, w_v, w_o):
        t = self.tokens
        left, right = w_o()
        cut = left.shape[1]
        dproj = (self.rows(2) * dout).astype(BF)
        datt = (nt(dproj[:, :cut], left) + nt(dproj[:, cut:], right)).astype(BF)
        dprobs = nt(datt, self.v_big)
        dv = self.fold(tn(self.probs, datt)).astype(BF)
        factor = self.head ** (-0.5)
        ds = []
        for h in range(LOCAL_HEADS):
            dp = dprobs[:, h * t : (h + 1) * t].astype(BF).astype(F32)
            p = self.probs32[h]
            ds.append((p * (dp - jnp.sum(p * dp, axis=-1, keepdims=True)) * factor).astype(BF))
        ds = jnp.concatenate(ds, axis=1)
        dqn = nn(ds, self.kn_big).astype(BF).astype(F32)
        dkn = self.fold(tn(ds, self.qn)).astype(BF).astype(F32)

        def norm_back(d, x, r):
            xn = x * r
            return r * (d - xn * self.to_lanes(self.per_head(d * xn)))

        dq = norm_back(dqn, self.q, self.r_q).astype(BF)
        dk = norm_back(dkn, self.k, self.r_k).astype(BF)
        dlow = (nt(dq, self.up_q) + nt(dv, self.up_v)).astype(BF)
        du = nt(dq, w_q()) + nt(dk, w_k()) + nt(dv, w_v()) + nn(dlow, self.down)
        du = du.astype(BF).astype(F32)
        grad_down = tn(dlow, self.u)
        grad_up = jnp.concatenate(
            [tn(self.low, dq)[: self.rank], tn(self.low, dv)[self.rank :]], axis=0
        )
        dn = du * (1.0 + self.rows(1))
        dz = dout + self.rstd * (
            dn
            - jnp.mean(dn, axis=-1, keepdims=True)
            - self.normed * jnp.mean(dn * self.normed, axis=-1, keepdims=True)
        )
        return dz, grad_down, grad_up


def spatial_mask(tokens, positions):
    row = lax.broadcasted_iota(jnp.int32, (tokens, tokens), 0)
    col = lax.broadcasted_iota(jnp.int32, (tokens, tokens), 1)
    return row // positions == col // positions


def temporal_mask(tokens, batch, positions):
    row = lax.broadcasted_iota(jnp.int32, (tokens, tokens), 0)
    col = lax.broadcasted_iota(jnp.int32, (tokens, tokens), 1)
    span = tokens // batch
    return (row // span == col // span) & (row % positions == col % positions)


def flip1(i):
    return i + 1 - 2 * (i % 2)


def flip2(i):
    return i + 2 - 4 * ((i // 2) % 2)


def layers_kernel(
    n_dp, n_seq, positions, z, upstream, mod, down, up, stack_s, stack_t, grad, down_s, up_s,
    down_t, up_t, w, sent_hidden, got_hidden, sent_back, got_back, own_sem, sib_send, sib_recv,
    a_send, a_recv, y_send, y_recv, z_send, z_recv, c_send, c_recv, f_send, f_recv, h_send,
    h_recv, b_send, b_recv,
):
    d, s = lax.axis_index("dp"), lax.axis_index("seq")
    chips = n_seq // 2
    chip, core = s // 2, s % 2
    sibling = (d, flip1(s))
    by_y, by_z = (flip1(d), s), (flip2(d), s)
    piece = d % 4
    hops = range(1, chips)

    def far(j):
        return 2 * lax.rem(chip + j + chips, chips) + core

    def seq_at(j):
        return lax.rem(s + j, n_seq)

    barrier = pltpu.get_barrier_semaphore()
    greet = [by_y, by_z] + [(d, seq_at(j)) for j in range(1, n_seq)]
    for target in greet:
        pl.semaphore_signal(barrier, inc=1, device_id=target, device_id_type=MESH)
    pl.semaphore_wait(barrier, len(greet))

    def remote(source, dest, send, recv, target):
        return pltpu.make_async_remote_copy(
            src_ref=source, dst_ref=dest, send_sem=send, recv_sem=recv, device_id=target,
            device_id_type=MESH,
        )

    stacks = (stack_s, stack_t)

    def own(l):
        return pltpu.make_async_copy(stacks[l], w.at[l, :, s], own_sem.at[l])

    def to_sibling(l):
        return remote(stacks[l], w.at[l, :, s], sib_send.at[l], sib_recv.at[l], sibling)

    def across(l, j):
        return remote(
            stacks[l].at[piece], w.at[l, piece, s], a_send.at[l, j - 1], a_recv.at[l, j - 1],
            (d, far(j)),
        )

    def pass_on(l, j, which, send, recv, target):
        held = w.at[l, which, far(-j)]
        return remote(held, held, send, recv, target)

    def to_y(l, j):
        return pass_on(l, j, piece, y_send.at[l, j - 1], y_recv.at[l, j - 1], by_y)

    def to_z(l, j):
        return pass_on(l, j, piece, z_send.at[l, j - 1], z_recv.at[l, j - 1], by_z)

    corner_piece = jnp.where(core == 0, flip2(piece), flip1(piece))
    corner_target = (jnp.where(core == 0, flip1(d), flip2(d)), s)

    def to_corner(l, j):
        return pass_on(
            l, j, corner_piece, c_send.at[l, j - 1], c_recv.at[l, j - 1], corner_target
        )

    kinds = [piece, flip1(piece), flip2(piece), flip1(flip2(piece))]

    def to_core(l, j, kind):
        return pass_on(
            l, j, kinds[kind], f_send.at[l, j - 1, kind], f_recv.at[l, j - 1, kind], sibling
        )

    def stage_first(l):
        for j in hops:
            across(l, j).start()

    def stage_near(l):
        to_sibling(l).start()
        own(l).start()

    def stage_pass(l):
        for j in hops:
            across(l, j).wait_recv()
            to_y(l, j).start()
            to_z(l, j).start()
            to_core(l, j, 0).start()

    def stage_corner(l):
        for j in hops:
            to_y(l, j).wait_recv()
            to_z(l, j).wait_recv()
            to_corner(l, j).start()
            to_core(l, j, 1).start()
            to_core(l, j, 2).start()

    def stage_last(l):
        for j in hops:
            to_corner(l, j).wait_recv()
            to_core(l, j, 3).start()
        for j in hops:
            for kind in range(4):
                to_core(l, j, kind).wait_recv()
        to_sibling(l).wait_recv()
        own(l).wait()

    inner = up.shape[3]
    lanes = w.shape[4]
    width = z.shape[1]
    out_rows = w.shape[3] // 2

    def loader(l, i):
        return lambda: jnp.concatenate([w[l, i, k, :, :inner] for k in range(n_seq)], axis=0)

    def out_loader(l):
        def load():
            left = [w[l, 3, k, :out_rows, :] for k in range(n_seq)]
            right = [w[l, 3, k, out_rows:, : width - lanes] for k in range(n_seq)]
            return jnp.concatenate(left, axis=0), jnp.concatenate(right, axis=0)

        return load

    def exchange(values, sent, got, send, recv):
        batch, blocks, span = sent.shape[:3]
        for b in range(batch):
            for k in range(blocks):
                start = (b * blocks + k) * span
                sent[b, k] = values[start : start + span].astype(BF)
        copies = [
            remote(
                sent.at[:, seq_at(j)], got.at[:, s], send.at[j - 1], recv.at[j - 1],
                (d, seq_at(j)),
            )
            for j in range(1, n_seq)
        ]
        for copy in copies:
            copy.start()
        got[:, s] = sent[:, s]
        return copies

    def received(copies, got):
        for copy in copies:
            copy.wait_recv()
        return jnp.concatenate(
            [
                got[b, k].astype(F32)
                for b in range(got.shape[0])
                for k in range(got.shape[1])
            ],
            axis=0,
        )

    stage_first(0)
    stage_near(0)
    tokens = z.shape[0]
    first = Layer(z[...], mod, 0, down, up, 0, spatial_mask(tokens, positions))
    stage_pass(0)
    stage_first(1)
    stage_near(1)
    stage_corner(0)
    stage_pass(1)
    stage_last(0)
    weights_s = [loader(0, i) for i in range(3)]
    first.project(*weights_s)
    first.attend()
    hidden = first.output(out_loader(0))
    out_copies = exchange(hidden, sent_hidden, got_hidden, h_send, h_recv)
    stage_corner(1)
    by_position = received(out_copies, got_hidden)
    second = Layer(
        by_position, mod, 3, down, up, 1,
        temporal_mask(tokens, mod.shape[0], got_hidden.shape[2]),
    )
    stage_last(1)
    weights_t = [loader(1, i) for i in range(3)]
    second.project(*weights_t)
    second.attend()
    back, down_t[...], up_t[...] = second.backward(
        upstream[...].astype(F32), *weights_t, out_loader(1)
    )
    back_copies = exchange(back, sent_back, got_back, b_send, b_recv)
    by_frame = received(back_copies, got_back)
    result, down_s[...], up_s[...] = first.backward(by_frame, *weights_s, out_loader(0))
    grad[...] = result.astype(BF)
    for copy in out_copies + back_copies:
        copy.wait_send()
    for l in range(2):
        to_sibling(l).wait_send()
        for j in hops:
            across(l, j).wait_send()
            to_y(l, j).wait_send()
            to_z(l, j).wait_send()
            to_corner(l, j).wait_send()
            for kind in range(4):
                to_core(l, j, kind).wait_send()


def stacked(w_in, w_out, lanes):
    left, right = w_out[:, :lanes], w_out[:, lanes:]
    right = jnp.pad(right, ((0, 0), (0, lanes - right.shape[1])))
    w_in = jnp.pad(w_in, ((0, 0), (0, 0), (0, lanes - w_in.shape[2])))
    return jnp.concatenate([w_in, jnp.concatenate([left, right], axis=0)[None]], axis=0)


def sum_kernel(
    n_dp, n_seq, x, out, wide, got_seq, part, got_dp, full, s1, r1, s2, r2, s3, r3, s4, r4
):
    d, s = lax.axis_index("dp"), lax.axis_index("seq")

    def seq_at(j):
        return lax.rem(s + j, n_seq)

    def dp_at(j):
        return lax.rem(d + j, n_dp)

    barrier = pltpu.get_barrier_semaphore()
    for j in range(1, n_seq):
        pl.semaphore_signal(barrier, inc=1, device_id=(d, seq_at(j)), device_id_type=MESH)
    for j in range(1, n_dp):
        pl.semaphore_signal(barrier, inc=1, device_id=(dp_at(j), s), device_id_type=MESH)
    wide[...] = x[...].astype(BF)
    pl.semaphore_wait(barrier, n_seq - 1 + n_dp - 1)

    def exchange(count, source, dest, send, recv, target):
        copies = [
            pltpu.make_async_remote_copy(
                src_ref=source(j), dst_ref=dest(j), send_sem=send.at[j - 1],
                recv_sem=recv.at[j - 1], device_id=target(j), device_id_type=MESH,
            )
            for j in range(1, count)
        ]
        for copy in copies:
            copy.start()
        return copies

    to_seq = lambda j: (d, seq_at(j))
    to_dp = lambda j: (dp_at(j), s)
    pending = exchange(
        n_seq, lambda j: wide.at[seq_at(j)], lambda j: got_seq.at[j - 1], s1, r1, to_seq
    )
    for copy in pending:
        copy.wait_recv()
    total = x[s]
    for j in range(1, n_seq):
        total = total + got_seq[j - 1].astype(F32)
    part[...] = total.astype(BF)
    more = exchange(n_dp, lambda j: part.at[dp_at(j)], lambda j: got_dp.at[j - 1], s2, r2, to_dp)
    for copy in more:
        copy.wait_recv()
    mine = part[d].astype(F32)
    for j in range(1, n_dp):
        mine = mine + got_dp[j - 1].astype(F32)
    full[s, d] = mine.astype(BF)
    pending += more
    more = exchange(n_dp, lambda j: full.at[s, d], lambda j: full.at[s, d], s3, r3, to_dp)
    for copy in more:
        copy.wait_recv()
    pending += more
    more = exchange(n_seq, lambda j: full.at[s], lambda j: full.at[s], s4, r4, to_seq)
    for copy in more:
        copy.wait_recv()
    out[...] = full[...].astype(F32)
    for copy in pending + more:
        copy.wait_send()


def sum_everywhere(n_dp, n_seq, flat):
    total = flat.shape[0]
    unit = 16 * 128
    devices = n_dp * n_seq
    rows = -(-total // (devices * unit)) * 16
    padded = jnp.pad(flat, (0, devices * rows * 128 - total))
    shape = (n_seq, n_dp, rows, 128)
    dma = pltpu.SemaphoreType.DMA
    seq_sem, dp_sem = dma((n_seq - 1,)), dma((n_dp - 1,))
    summed = pl.pallas_call(
        functools.partial(sum_kernel, n_dp, n_seq),
        out_shape=jax.ShapeDtypeStruct(shape, F32),
        in_specs=[VMEM],
        out_specs=VMEM,
        scratch_shapes=[
            pltpu.VMEM(shape, BF),
            pltpu.VMEM((n_seq - 1,) + shape[1:], BF),
            pltpu.VMEM(shape[1:], BF),
            pltpu.VMEM((n_dp - 1,) + shape[2:], BF),
            pltpu.VMEM(shape, BF),
            seq_sem, seq_sem, dp_sem, dp_sem, dp_sem, dp_sem, seq_sem, seq_sem,
        ],
        compiler_params=pltpu.CompilerParams(
            collective_id=1, has_side_effects=True, vmem_limit_bytes=VMEM_BYTES
        ),
    )(padded.reshape(shape))
    return summed.reshape(-1)[:total]


def per_device(n_dp, n_seq, z, upstream, mod, in_s, out_s, in_t, out_t, down, up):
    batch, frames_here, positions, width = z.shape
    frames = frames_here * n_seq
    span = positions // n_seq
    inner, rank = up.shape[3], up.shape[2]
    tokens = batch * frames_here * positions
    factor = float(batch * n_dp * frames * positions) ** (-0.5)
    lanes = -(-inner // 128) * 128
    links = max(n_seq // 2 - 1, 1)
    shape = jax.ShapeDtypeStruct
    dma = pltpu.SemaphoreType.DMA
    buffer = pltpu.VMEM((batch, n_seq, span, width), BF)
    pair, hop, lane = dma((2,)), dma((2, links)), dma((n_seq - 1,))
    grads = [shape((2 * rank, width), F32), shape((2 * rank, inner), F32)]
    grad, down_s, up_s, down_t, up_t = pl.pallas_call(
        functools.partial(layers_kernel, n_dp, n_seq, positions),
        out_shape=[shape((tokens, width), BF)] + grads * 2,
        in_specs=[VMEM] * 5 + [ANY] * 2,
        out_specs=[VMEM] * 5,
        scratch_shapes=[pltpu.VMEM((2, 4, n_seq) + (in_s.shape[1], lanes), BF)]
        + [buffer] * 4
        + [pair] * 3
        + [hop] * 8
        + [dma((2, links, 4))] * 2
        + [lane] * 4,
        compiler_params=pltpu.CompilerParams(
            collective_id=0, has_side_effects=True, vmem_limit_bytes=VMEM_BYTES
        ),
    )(
        z.reshape(tokens, width), upstream.reshape(tokens, width), mod, down, up,
        stacked(in_s, out_s, lanes), stacked(in_t, out_t, lanes),
    )
    flat = jnp.concatenate([a.reshape(-1) for a in (down_s, down_t, up_s, up_t)]) * factor
    flat = sum_everywhere(n_dp, n_seq, flat)
    cut = down.size
    return grad.reshape(z.shape), flat[:cut].reshape(down.shape), flat[cut:].reshape(up.shape)


def solution(mesh):
    placed = (
        P("dp", "seq", None, None),
        P("dp", None, "seq", None),
        P("dp", None, None),
        P(None, "seq", None),
        P("seq", None),
        P(None, "seq", None),
        P("seq", None),
        P(),
        P(),
    )
    return jax.shard_map(
        functools.partial(per_device, mesh.shape["dp"], mesh.shape["seq"]),
        mesh=mesh,
        in_specs=placed,
        out_specs=(P("dp", "seq", None, None), P(), P()),
        check_vma=False,
    )
```

```python
import functools

import jax
import jax.numpy as jnp
from jax import lax
from jax.experimental import pallas as pl
from jax.experimental.pallas import tpu as pltpu
from jax.sharding import PartitionSpec as P

LOCAL_HEADS = 8
EPSILON = 1e-06
MESH = pl.DeviceIdType.MESH
BF, F32 = jnp.bfloat16, jnp.float32
VMEM = pl.BlockSpec(memory_space=pltpu.VMEM)
ANY = pl.BlockSpec(memory_space=pl.ANY)
VMEM_BYTES = 56 * 2**20


def nn(a, b):
    return lax.dot_general(a, b, (((1,), (0,)), ((), ())), preferred_element_type=F32)


def nt(a, b):
    return lax.dot_general(a, b, (((1,), (1,)), ((), ())), preferred_element_type=F32)


def tn(a, b):
    return lax.dot_general(a, b, (((0,), (0,)), ((), ())), preferred_element_type=F32)


def nt_full(a, b):
    return lax.dot_general(
        a, b, (((1,), (1,)), ((), ())), preferred_element_type=F32, precision=lax.Precision.HIGHEST
    )


def nn_full(a, b):
    return lax.dot_general(
        a, b, (((1,), (0,)), ((), ())), preferred_element_type=F32, precision=lax.Precision.HIGHEST
    )


class Layer:
    def __init__(self, z, mod_ref, row, down_ref, up_ref, layer, group_mask):
        self.tokens, self.width = z.shape
        self.batch = mod_ref.shape[0]
        self.mod_ref, self.row = mod_ref, row
        self.z = z.astype(F32)
        center = self.z - jnp.mean(self.z, axis=-1, keepdims=True)
        self.rstd = lax.rsqrt(jnp.mean(center * center, axis=-1, keepdims=True) + EPSILON)
        self.normed = center * self.rstd
        self.u = (self.normed * (1.0 + self.rows(1)) + self.rows(0)).astype(BF)
        rank = down_ref.shape[2]
        inner = up_ref.shape[3]
        self.rank, self.inner = rank, inner
        self.down = down_ref[layer].reshape(2 * rank, self.width).astype(BF)
        zero = jnp.zeros((rank, inner), BF)
        self.up_q = jnp.concatenate([up_ref[layer, 0].astype(BF), zero], axis=0)
        self.up_v = jnp.concatenate([zero, up_ref[layer, 1].astype(BF)], axis=0)
        self.head = inner // LOCAL_HEADS
        lane_head = lax.broadcasted_iota(jnp.int32, (1, inner), 1) // self.head
        self.head_rows = [(lane_head == h).astype(F32).astype(BF) for h in range(LOCAL_HEADS)]
        self.head_rows32 = [(lane_head == h).astype(F32) for h in range(LOCAL_HEADS)]
        spread_head = lax.broadcasted_iota(jnp.int32, (128, inner), 1) // self.head
        spread_row = lax.broadcasted_iota(jnp.int32, (128, inner), 0)
        self.spread = (spread_head == spread_row).astype(F32)
        self.group_mask = group_mask

    def rows(self, j):
        span = self.tokens // self.batch
        return jnp.concatenate(
            [
                jnp.broadcast_to(self.mod_ref[b, self.row + j][None, :], (span, self.width))
                for b in range(self.batch)
            ],
            axis=0,
        )

    def per_head(self, values):
        return nt_full(values, self.spread) * (1.0 / self.head)

    def to_lanes(self, values):
        return nn_full(values, self.spread)

    def big(self, values):
        return jnp.concatenate([values * m for m in self.head_rows], axis=0)

    def fold(self, values):
        t = self.tokens
        return sum(
            values[h * t : (h + 1) * t] * self.head_rows32[h] for h in range(LOCAL_HEADS)
        )

    def project(self, w_q, w_k, w_v):
        self.low = nt(self.u, self.down).astype(BF)
        self.q = nn(self.u, w_q()) + nn(self.low, self.up_q)
        self.k = nn(self.u, w_k())
        self.v = (nn(self.u, w_v()) + nn(self.low, self.up_v)).astype(BF)

    def attend(self):
        t = self.tokens
        self.r_q = self.to_lanes(lax.rsqrt(self.per_head(self.q * self.q) + EPSILON))
        self.r_k = self.to_lanes(lax.rsqrt(self.per_head(self.k * self.k) + EPSILON))
        self.qn = (self.q * self.r_q).astype(BF)
        self.kn_big = self.big((self.k * self.r_k).astype(BF))
        self.v_big = self.big(self.v)
        scores = nt(self.qn, self.kn_big)
        factor = self.head ** (-0.5)
        probs = []
        for h in range(LOCAL_HEADS):
            e = jnp.where(self.group_mask, jnp.exp(scores[:, h * t : (h + 1) * t] * factor), 0.0)
            probs.append(e / jnp.sum(e, axis=-1, keepdims=True))
        self.probs32 = probs
        self.probs = jnp.concatenate([p.astype(BF) for p in probs], axis=1)

    def output(self, w_o):
        att = nn(self.probs, self.v_big).astype(BF)
        left, right = w_o()
        projected = jnp.concatenate([nn(att, left), nn(att, right)], axis=1)
        return self.z + self.rows(2) * projected

    def backward(self, dout, w_q, w_k, w_v, w_o):
        t = self.tokens
        left, right = w_o()
        cut = left.shape[1]
        dproj = (self.rows(2) * dout).astype(BF)
        datt = (nt(dproj[:, :cut], left) + nt(dproj[:, cut:], right)).astype(BF)
        dprobs = nt(datt, self.v_big)
        dv = self.fold(tn(self.probs, datt)).astype(BF)
        factor = self.head ** (-0.5)
        ds = []
        for h in range(LOCAL_HEADS):
            dp = dprobs[:, h * t : (h + 1) * t].astype(BF).astype(F32)
            p = self.probs32[h]
            ds.append((p * (dp - jnp.sum(p * dp, axis=-1, keepdims=True)) * factor).astype(BF))
        ds = jnp.concatenate(ds, axis=1)
        dqn = nn(ds, self.kn_big).astype(BF).astype(F32)
        dkn = self.fold(tn(ds, self.qn)).astype(BF).astype(F32)

        def norm_back(d, x, r):
            xn = x * r
            return r * (d - xn * self.to_lanes(self.per_head(d * xn)))

        dq = norm_back(dqn, self.q, self.r_q).astype(BF)
        dk = norm_back(dkn, self.k, self.r_k).astype(BF)
        dlow = (nt(dq, self.up_q) + nt(dv, self.up_v)).astype(BF)
        du = nt(dq, w_q()) + nt(dk, w_k()) + nt(dv, w_v()) + nn(dlow, self.down)
        du = du.astype(BF).astype(F32)
        grad_down = tn(dlow, self.u)
        grad_up = jnp.concatenate(
            [tn(self.low, dq)[: self.rank], tn(self.low, dv)[self.rank :]], axis=0
        )
        dn = du * (1.0 + self.rows(1))
        dz = dout + self.rstd * (
            dn
            - jnp.mean(dn, axis=-1, keepdims=True)
            - self.normed * jnp.mean(dn * self.normed, axis=-1, keepdims=True)
        )
        return dz, grad_down, grad_up


def spatial_mask(tokens, positions):
    row = lax.broadcasted_iota(jnp.int32, (tokens, tokens), 0)
    col = lax.broadcasted_iota(jnp.int32, (tokens, tokens), 1)
    return row // positions == col // positions


def temporal_mask(tokens, batch, positions):
    row = lax.broadcasted_iota(jnp.int32, (tokens, tokens), 0)
    col = lax.broadcasted_iota(jnp.int32, (tokens, tokens), 1)
    span = tokens // batch
    return (row // span == col // span) & (row % positions == col % positions)


def flip1(i):
    return i + 1 - 2 * (i % 2)


def flip2(i):
    return i + 2 - 4 * ((i // 2) % 2)


def layers_kernel(
    n_dp, n_seq, positions, factor, z, upstream, mod, down, up, stack_s, stack_t, grad,
    all_down, all_up, w, wide, got_seq, part, got_dp, full, sent_hidden, got_hidden, sent_back, got_back, own_sem, sib_send, sib_recv,
    a_send, a_recv, y_send, y_recv, z_send, z_recv, c_send, c_recv, f_send, f_recv, h_send,
    h_recv, b_send, b_recv, s1, r1, s2, r2, s3, r3, s4, r4,
):
    d, s = lax.axis_index("dp"), lax.axis_index("seq")
    chips = n_seq // 2
    chip, core = s // 2, s % 2
    sibling = (d, flip1(s))
    by_y, by_z = (flip1(d), s), (flip2(d), s)
    piece = d % 4
    hops = range(1, chips)

    def far(j):
        return 2 * lax.rem(chip + j + chips, chips) + core

    def seq_at(j):
        return lax.rem(s + j, n_seq)

    def dp_at(j):
        return lax.rem(d + j, n_dp)

    barrier = pltpu.get_barrier_semaphore()
    greet = [(dp_at(j), s) for j in range(1, n_dp)] + [(d, seq_at(j)) for j in range(1, n_seq)]
    for target in greet:
        pl.semaphore_signal(barrier, inc=1, device_id=target, device_id_type=MESH)
    pl.semaphore_wait(barrier, len(greet))

    def remote(source, dest, send, recv, target):
        return pltpu.make_async_remote_copy(
            src_ref=source, dst_ref=dest, send_sem=send, recv_sem=recv, device_id=target,
            device_id_type=MESH,
        )

    stacks = (stack_s, stack_t)

    def own(l):
        return pltpu.make_async_copy(stacks[l], w.at[l, :, s], own_sem.at[l])

    def to_sibling(l):
        return remote(stacks[l], w.at[l, :, s], sib_send.at[l], sib_recv.at[l], sibling)

    def across(l, j):
        return remote(
            stacks[l].at[piece], w.at[l, piece, s], a_send.at[l, j - 1], a_recv.at[l, j - 1],
            (d, far(j)),
        )

    def pass_on(l, j, which, send, recv, target):
        held = w.at[l, which, far(-j)]
        return remote(held, held, send, recv, target)

    def to_y(l, j):
        return pass_on(l, j, piece, y_send.at[l, j - 1], y_recv.at[l, j - 1], by_y)

    def to_z(l, j):
        return pass_on(l, j, piece, z_send.at[l, j - 1], z_recv.at[l, j - 1], by_z)

    corner_piece = jnp.where(core == 0, flip2(piece), flip1(piece))
    corner_target = (jnp.where(core == 0, flip1(d), flip2(d)), s)

    def to_corner(l, j):
        return pass_on(
            l, j, corner_piece, c_send.at[l, j - 1], c_recv.at[l, j - 1], corner_target
        )

    kinds = [piece, flip1(piece), flip2(piece), flip1(flip2(piece))]

    def to_core(l, j, kind):
        return pass_on(
            l, j, kinds[kind], f_send.at[l, j - 1, kind], f_recv.at[l, j - 1, kind], sibling
        )

    def stage_first(l):
        for j in hops:
            across(l, j).start()

    def stage_near(l):
        to_sibling(l).start()
        own(l).start()

    def stage_pass(l):
        for j in hops:
            across(l, j).wait_recv()
            to_y(l, j).start()
            to_z(l, j).start()
            to_core(l, j, 0).start()

    def stage_corner(l):
        for j in hops:
            to_y(l, j).wait_recv()
            to_z(l, j).wait_recv()
            to_corner(l, j).start()
            to_core(l, j, 1).start()
            to_core(l, j, 2).start()

    def stage_last(l):
        for j in hops:
            to_corner(l, j).wait_recv()
            to_core(l, j, 3).start()
        for j in hops:
            for kind in range(4):
                to_core(l, j, kind).wait_recv()
        to_sibling(l).wait_recv()
        own(l).wait()

    inner = up.shape[3]
    lanes = w.shape[4]
    width = z.shape[1]
    out_rows = w.shape[3] // 2

    def loader(l, i):
        return lambda: jnp.concatenate([w[l, i, k, :, :inner] for k in range(n_seq)], axis=0)

    def out_loader(l):
        def load():
            left = [w[l, 3, k, :out_rows, :] for k in range(n_seq)]
            right = [w[l, 3, k, out_rows:, : width - lanes] for k in range(n_seq)]
            return jnp.concatenate(left, axis=0), jnp.concatenate(right, axis=0)

        return load

    def exchange(values, sent, got, send, recv):
        batch, blocks, span = sent.shape[:3]
        for b in range(batch):
            for k in range(blocks):
                start = (b * blocks + k) * span
                sent[b, k] = values[start : start + span].astype(BF)
        copies = [
            remote(
                sent.at[:, seq_at(j)], got.at[:, s], send.at[j - 1], recv.at[j - 1],
                (d, seq_at(j)),
            )
            for j in range(1, n_seq)
        ]
        for copy in copies:
            copy.start()
        got[:, s] = sent[:, s]
        return copies

    def received(copies, got):
        for copy in copies:
            copy.wait_recv()
        return jnp.concatenate(
            [
                got[b, k].astype(F32)
                for b in range(got.shape[0])
                for k in range(got.shape[1])
            ],
            axis=0,
        )

    part_rows = wide.shape[3]
    block_parts = down.shape[2] * 2 // part_rows
    down_blocks = width // 128
    up_blocks = -(-inner // 128)
    used = (down_blocks + up_blocks) * block_parts
    all_sends = []

    def spot(p):
        return p // n_dp, p % n_dp

    def fan(count, source, dest, send, recv, target):
        copies = [
            remote(source(j), dest(j), send.at[j - 1], recv.at[j - 1], target(j))
            for j in range(1, count)
        ]
        for copy in copies:
            copy.start()
        all_sends.extend(copies)
        return copies

    def to_seq(j):
        return d, seq_at(j)

    def to_dp(j):
        return dp_at(j), s

    def landed(copies):
        for copy in copies:
            copy.wait_recv()

    def sum_first(l, grad_down, grad_up):
        fill = jnp.zeros((grad_up.shape[0], up_blocks * 128 - inner), F32)
        grad_up = jnp.concatenate([grad_up, fill], axis=1)
        for p in range(n_dp * n_seq):
            i, k = spot(p)
            if p >= used:
                wide[l, i, k] = jnp.zeros((part_rows, 128), BF)
                continue
            c, h = p // block_parts, p % block_parts
            values = grad_down if c < down_blocks else grad_up
            c = c if c < down_blocks else c - down_blocks
            rows = values[h * part_rows : (h + 1) * part_rows, c * 128 : (c + 1) * 128]
            wide[l, i, k] = rows.astype(BF)
        return fan(
            n_seq, lambda j: wide.at[l, seq_at(j)], lambda j: got_seq.at[l, j - 1],
            s1.at[l], r1.at[l], to_seq,
        )

    def sum_second(l, copies):
        landed(copies)
        total = wide[l, s].astype(F32)
        for j in range(1, n_seq):
            total = total + got_seq[l, j - 1].astype(F32)
        part[l] = total.astype(BF)
        return fan(
            n_dp, lambda j: part.at[l, dp_at(j)], lambda j: got_dp.at[l, j - 1],
            s2.at[l], r2.at[l], to_dp,
        )

    def sum_third(l, copies):
        landed(copies)
        total = part[l, d].astype(F32)
        for j in range(1, n_dp):
            total = total + got_dp[l, j - 1].astype(F32)
        full[l, s, d] = total.astype(BF)
        return fan(
            n_dp, lambda j: full.at[l, s, d], lambda j: full.at[l, s, d],
            s3.at[l], r3.at[l], to_dp,
        )

    def sum_fourth(l, copies):
        landed(copies)
        return fan(
            n_seq, lambda j: full.at[l, s], lambda j: full.at[l, s], s4.at[l], r4.at[l], to_seq
        )

    def sum_last(l, copies):
        landed(copies)
        for p in range(used):
            i, k = spot(p)
            c, h = p // block_parts, p % block_parts
            rows = pl.ds(h * part_rows, part_rows)
            values = full[l, i, k].astype(F32) * factor
            if c < down_blocks:
                all_down[l, rows, c * 128 : (c + 1) * 128] = values
            else:
                start = (c - down_blocks) * 128
                stop = min(start + 128, inner)
                all_up[l, rows, start:stop] = values[:, : stop - start]

    stage_first(0)
    stage_near(0)
    tokens = z.shape[0]
    first = Layer(z[...], mod, 0, down, up, 0, spatial_mask(tokens, positions))
    stage_pass(0)
    stage_first(1)
    stage_near(1)
    stage_corner(0)
    stage_pass(1)
    stage_last(0)
    weights_s = [loader(0, i) for i in range(3)]
    first.project(*weights_s)
    first.attend()
    hidden = first.output(out_loader(0))
    out_copies = exchange(hidden, sent_hidden, got_hidden, h_send, h_recv)
    stage_corner(1)
    by_position = received(out_copies, got_hidden)
    second = Layer(
        by_position, mod, 3, down, up, 1,
        temporal_mask(tokens, mod.shape[0], got_hidden.shape[2]),
    )
    stage_last(1)
    weights_t = [loader(1, i) for i in range(3)]
    second.project(*weights_t)
    second.attend()
    back, down_t, up_t = second.backward(
        upstream[...].astype(F32), *weights_t, out_loader(1)
    )
    back_copies = exchange(back, sent_back, got_back, b_send, b_recv)
    sum_t = sum_first(1, down_t, up_t)
    by_frame = received(back_copies, got_back)
    sum_t = sum_second(1, sum_t)
    result, down_s, up_s = first.backward(by_frame, *weights_s, out_loader(0))
    sum_s = sum_first(0, down_s, up_s)
    sum_t = sum_third(1, sum_t)
    grad[...] = result.astype(BF)
    sum_s = sum_second(0, sum_s)
    sum_t = sum_fourth(1, sum_t)
    sum_s = sum_third(0, sum_s)
    sum_s = sum_fourth(0, sum_s)
    sum_last(1, sum_t)
    sum_last(0, sum_s)
    for copy in out_copies + back_copies + all_sends:
        copy.wait_send()
    for l in range(2):
        to_sibling(l).wait_send()
        for j in hops:
            across(l, j).wait_send()
            to_y(l, j).wait_send()
            to_z(l, j).wait_send()
            to_corner(l, j).wait_send()
            for kind in range(4):
                to_core(l, j, kind).wait_send()


def stacked(w_in, w_out, lanes):
    left, right = w_out[:, :lanes], w_out[:, lanes:]
    right = jnp.pad(right, ((0, 0), (0, lanes - right.shape[1])))
    w_in = jnp.pad(w_in, ((0, 0), (0, 0), (0, lanes - w_in.shape[2])))
    return jnp.concatenate([w_in, jnp.concatenate([left, right], axis=0)[None]], axis=0)


def per_device(n_dp, n_seq, z, upstream, mod, in_s, out_s, in_t, out_t, down, up):
    batch, frames_here, positions, width = z.shape
    frames = frames_here * n_seq
    span = positions // n_seq
    inner, rank = up.shape[3], up.shape[2]
    tokens = batch * frames_here * positions
    factor = float(batch * n_dp * frames * positions) ** (-0.5)
    lanes = -(-inner // 128) * 128
    links = max(n_seq // 2 - 1, 1)
    shape = jax.ShapeDtypeStruct
    dma = pltpu.SemaphoreType.DMA
    buffer = pltpu.VMEM((batch, n_seq, span, width), BF)
    pair, hop, lane = dma((2,)), dma((2, links)), dma((n_seq - 1,))
    grads = [shape((2, 2 * rank, width), F32), shape((2, 2 * rank, inner), F32)]
    needed = 2 * rank * (width // 128 + -(-inner // 128))
    part_rows = 16
    while part_rows * n_dp * n_seq < needed:
        part_rows *= 2
    part = (part_rows, 128)
    seq_sem, dp_sem = dma((2, n_seq - 1)), dma((2, n_dp - 1))
    grad, all_down, all_up = pl.pallas_call(
        functools.partial(layers_kernel, n_dp, n_seq, positions, factor),
        out_shape=[shape((tokens, width), BF)] + grads,
        in_specs=[VMEM] * 5 + [ANY] * 2,
        out_specs=[VMEM] * 3,
        scratch_shapes=[pltpu.VMEM((2, 4, n_seq) + (in_s.shape[1], lanes), BF)]
        + [
            pltpu.VMEM((2,) + lead + part, BF)
            for lead in ((n_seq, n_dp), (n_seq - 1, n_dp), (n_dp,), (n_dp - 1,), (n_seq, n_dp))
        ]
        + [buffer] * 4
        + [pair] * 3
        + [hop] * 8
        + [dma((2, links, 4))] * 2
        + [lane] * 4
        + [seq_sem] * 2
        + [dp_sem] * 4
        + [seq_sem] * 2,
        compiler_params=pltpu.CompilerParams(
            collective_id=0, has_side_effects=True, vmem_limit_bytes=VMEM_BYTES
        ),
    )(
        z.reshape(tokens, width), upstream.reshape(tokens, width), mod, down, up,
        stacked(in_s, out_s, lanes), stacked(in_t, out_t, lanes),
    )
    return grad.reshape(z.shape), all_down.reshape(down.shape), all_up.reshape(up.shape)


def solution(mesh):
    placed = (
        P("dp", "seq", None, None),
        P("dp", None, "seq", None),
        P("dp", None, None),
        P(None, "seq", None),
        P("seq", None),
        P(None, "seq", None),
        P("seq", None),
        P(),
        P(),
    )
    return jax.shard_map(
        functools.partial(per_device, mesh.shape["dp"], mesh.shape["seq"]),
        mesh=mesh,
        in_specs=placed,
        out_specs=(P("dp", "seq", None, None), P(), P()),
        check_vma=False,
    )
```

```python
import functools

import jax
import jax.numpy as jnp
from jax import lax
from jax.experimental import pallas as pl
from jax.experimental.pallas import tpu as pltpu
from jax.sharding import PartitionSpec as P

LOCAL_HEADS = 8
EPSILON = 1e-06
MESH = pl.DeviceIdType.MESH
BF, F32 = jnp.bfloat16, jnp.float32
VMEM = pl.BlockSpec(memory_space=pltpu.VMEM)
ANY = pl.BlockSpec(memory_space=pl.ANY)
VMEM_BYTES = 56 * 2**20


def nn(a, b):
    return lax.dot_general(a, b, (((1,), (0,)), ((), ())), preferred_element_type=F32)


def nt(a, b):
    return lax.dot_general(a, b, (((1,), (1,)), ((), ())), preferred_element_type=F32)


def tn(a, b):
    return lax.dot_general(a, b, (((0,), (0,)), ((), ())), preferred_element_type=F32)


def nt_full(a, b):
    return lax.dot_general(
        a, b, (((1,), (1,)), ((), ())), preferred_element_type=F32, precision=lax.Precision.HIGHEST
    )


def nn_full(a, b):
    return lax.dot_general(
        a, b, (((1,), (0,)), ((), ())), preferred_element_type=F32, precision=lax.Precision.HIGHEST
    )


class Layer:
    def __init__(self, z, mod_ref, row, down_ref, up_ref, layer, group_mask):
        self.tokens, self.width = z.shape
        self.batch = mod_ref.shape[0]
        self.mod_ref, self.row = mod_ref, row
        self.z = z.astype(F32)
        center = self.z - jnp.mean(self.z, axis=-1, keepdims=True)
        self.rstd = lax.rsqrt(jnp.mean(center * center, axis=-1, keepdims=True) + EPSILON)
        self.normed = center * self.rstd
        self.u = (self.normed * (1.0 + self.rows(1)) + self.rows(0)).astype(BF)
        rank = down_ref.shape[2]
        inner = up_ref.shape[3]
        self.rank, self.inner = rank, inner
        self.down = down_ref[layer].reshape(2 * rank, self.width).astype(BF)
        zero = jnp.zeros((rank, inner), BF)
        self.up_q = jnp.concatenate([up_ref[layer, 0].astype(BF), zero], axis=0)
        self.up_v = jnp.concatenate([zero, up_ref[layer, 1].astype(BF)], axis=0)
        self.head = inner // LOCAL_HEADS
        lane_head = lax.broadcasted_iota(jnp.int32, (1, inner), 1) // self.head
        self.head_rows = [(lane_head == h).astype(F32).astype(BF) for h in range(LOCAL_HEADS)]
        self.head_rows32 = [(lane_head == h).astype(F32) for h in range(LOCAL_HEADS)]
        spread_head = lax.broadcasted_iota(jnp.int32, (128, inner), 1) // self.head
        spread_row = lax.broadcasted_iota(jnp.int32, (128, inner), 0)
        self.spread = (spread_head == spread_row).astype(F32)
        self.group_mask = group_mask

    def rows(self, j):
        span = self.tokens // self.batch
        return jnp.concatenate(
            [
                jnp.broadcast_to(self.mod_ref[b, self.row + j][None, :], (span, self.width))
                for b in range(self.batch)
            ],
            axis=0,
        )

    def per_head(self, values):
        return nt_full(values, self.spread) * (1.0 / self.head)

    def to_lanes(self, values):
        return nn_full(values, self.spread)

    def big(self, values):
        return jnp.concatenate([values * m for m in self.head_rows], axis=0)

    def fold(self, values):
        t = self.tokens
        return sum(
            values[h * t : (h + 1) * t] * self.head_rows32[h] for h in range(LOCAL_HEADS)
        )

    def project(self, w_q, w_k, w_v):
        self.low = nt(self.u, self.down).astype(BF)
        self.q = nn(self.u, w_q()) + nn(self.low, self.up_q)
        self.k = nn(self.u, w_k())
        self.v = (nn(self.u, w_v()) + nn(self.low, self.up_v)).astype(BF)

    def attend(self):
        t = self.tokens
        self.r_q = self.to_lanes(lax.rsqrt(self.per_head(self.q * self.q) + EPSILON))
        self.r_k = self.to_lanes(lax.rsqrt(self.per_head(self.k * self.k) + EPSILON))
        self.qn = (self.q * self.r_q).astype(BF)
        self.kn_big = self.big((self.k * self.r_k).astype(BF))
        self.v_big = self.big(self.v)
        scores = nt(self.qn, self.kn_big)
        factor = self.head ** (-0.5)
        probs = []
        for h in range(LOCAL_HEADS):
            e = jnp.where(self.group_mask, jnp.exp(scores[:, h * t : (h + 1) * t] * factor), 0.0)
            probs.append(e / jnp.sum(e, axis=-1, keepdims=True))
        self.probs32 = probs
        self.probs = jnp.concatenate([p.astype(BF) for p in probs], axis=1)

    def output(self, w_o):
        att = nn(self.probs, self.v_big).astype(BF)
        left, right = w_o()
        projected = jnp.concatenate([nn(att, left), nn(att, right)], axis=1)
        return self.z + self.rows(2) * projected

    def backward(self, dout, w_q, w_k, w_v, w_o):
        t = self.tokens
        left, right = w_o()
        cut = left.shape[1]
        dproj = (self.rows(2) * dout).astype(BF)
        datt = (nt(dproj[:, :cut], left) + nt(dproj[:, cut:], right)).astype(BF)
        dprobs = nt(datt, self.v_big)
        dv = self.fold(tn(self.probs, datt)).astype(BF)
        factor = self.head ** (-0.5)
        ds = []
        for h in range(LOCAL_HEADS):
            dp = dprobs[:, h * t : (h + 1) * t].astype(BF).astype(F32)
            p = self.probs32[h]
            ds.append((p * (dp - jnp.sum(p * dp, axis=-1, keepdims=True)) * factor).astype(BF))
        ds = jnp.concatenate(ds, axis=1)
        dqn = nn(ds, self.kn_big).astype(BF).astype(F32)
        dkn = self.fold(tn(ds, self.qn)).astype(BF).astype(F32)

        def norm_back(d, x, r):
            xn = x * r
            return r * (d - xn * self.to_lanes(self.per_head(d * xn)))

        dq = norm_back(dqn, self.q, self.r_q).astype(BF)
        dk = norm_back(dkn, self.k, self.r_k).astype(BF)
        dlow = (nt(dq, self.up_q) + nt(dv, self.up_v)).astype(BF)
        du = nt(dq, w_q()) + nt(dk, w_k()) + nt(dv, w_v()) + nn(dlow, self.down)
        du = du.astype(BF).astype(F32)
        grad_down = tn(dlow, self.u)
        grad_up = jnp.concatenate(
            [tn(self.low, dq)[: self.rank], tn(self.low, dv)[self.rank :]], axis=0
        )
        dn = du * (1.0 + self.rows(1))
        dz = dout + self.rstd * (
            dn
            - jnp.mean(dn, axis=-1, keepdims=True)
            - self.normed * jnp.mean(dn * self.normed, axis=-1, keepdims=True)
        )
        return dz, grad_down, grad_up


def spatial_mask(tokens, positions):
    row = lax.broadcasted_iota(jnp.int32, (tokens, tokens), 0)
    col = lax.broadcasted_iota(jnp.int32, (tokens, tokens), 1)
    return row // positions == col // positions


def temporal_mask(tokens, batch, positions):
    row = lax.broadcasted_iota(jnp.int32, (tokens, tokens), 0)
    col = lax.broadcasted_iota(jnp.int32, (tokens, tokens), 1)
    span = tokens // batch
    return (row // span == col // span) & (row % positions == col % positions)


def flip1(i):
    return i + 1 - 2 * (i % 2)


def flip2(i):
    return i + 2 - 4 * ((i // 2) % 2)


def layers_kernel(
    n_dp, n_seq, positions, factor, z, upstream, mod, down, up, stack_s, stack_t, grad,
    all_down, all_up, w, wide, got_seq, part, got_dp, full, sent_hidden, got_hidden, sent_back, got_back, own_sem, sib_send, sib_recv,
    a_send, a_recv, y_send, y_recv, z_send, z_recv, c_send, c_recv, f_send, f_recv, h_send,
    h_recv, b_send, b_recv, s1, r1, s2, r2, s3, r3, s4, r4,
):
    d, s = lax.axis_index("dp"), lax.axis_index("seq")
    chips = n_seq // 2
    chip, core = s // 2, s % 2
    sibling = (d, flip1(s))
    by_y, by_z = (flip1(d), s), (flip2(d), s)
    piece = d % 4
    cuts = 2 if w.shape[3] % 32 == 0 else 1
    rows_each = w.shape[3] // cuts
    hops = range(cuts, chips * cuts)

    def span_of(j):
        return pl.ds(j % cuts * rows_each, rows_each)

    def far(j):
        return 2 * lax.rem(chip + j + chips, chips) + core

    def seq_at(j):
        return lax.rem(s + j, n_seq)

    def dp_at(j):
        return lax.rem(d + j, n_dp)

    barrier = pltpu.get_barrier_semaphore()
    greet = [(dp_at(j), s) for j in range(1, n_dp)] + [(d, seq_at(j)) for j in range(1, n_seq)]
    for target in greet:
        pl.semaphore_signal(barrier, inc=1, device_id=target, device_id_type=MESH)
    pl.semaphore_wait(barrier, len(greet))

    def remote(source, dest, send, recv, target):
        return pltpu.make_async_remote_copy(
            src_ref=source, dst_ref=dest, send_sem=send, recv_sem=recv, device_id=target,
            device_id_type=MESH,
        )

    stacks = (stack_s, stack_t)

    def own(l):
        return pltpu.make_async_copy(stacks[l], w.at[l, :, s], own_sem.at[l])

    def to_sibling(l):
        return remote(stacks[l], w.at[l, :, s], sib_send.at[l], sib_recv.at[l], sibling)

    def across(l, j):
        return remote(
            stacks[l].at[piece, span_of(j)], w.at[l, piece, s, span_of(j)],
            a_send.at[l, j - cuts], a_recv.at[l, j - cuts], (d, far(j // cuts)),
        )

    def pass_on(l, j, which, send, recv, target):
        held = w.at[l, which, far(-(j // cuts)), span_of(j)]
        return remote(held, held, send, recv, target)

    def to_y(l, j):
        return pass_on(l, j, piece, y_send.at[l, j - cuts], y_recv.at[l, j - cuts], by_y)

    def to_z(l, j):
        return pass_on(l, j, piece, z_send.at[l, j - cuts], z_recv.at[l, j - cuts], by_z)

    corner_piece = jnp.where(core == 0, flip2(piece), flip1(piece))
    corner_target = (jnp.where(core == 0, flip1(d), flip2(d)), s)

    def to_corner(l, j):
        return pass_on(
            l, j, corner_piece, c_send.at[l, j - cuts], c_recv.at[l, j - cuts], corner_target
        )

    kinds = [piece, flip1(piece), flip2(piece), flip1(flip2(piece))]

    def to_core(l, j, kind):
        return pass_on(
            l, j, kinds[kind], f_send.at[l, j - cuts, kind], f_recv.at[l, j - cuts, kind], sibling
        )

    def stage_first(l):
        for j in hops:
            across(l, j).start()

    def stage_near(l):
        to_sibling(l).start()
        own(l).start()

    def stage_pass(l):
        for j in hops:
            across(l, j).wait_recv()
            to_y(l, j).start()
            to_z(l, j).start()
            to_core(l, j, 0).start()

    def stage_corner(l):
        for j in hops:
            to_y(l, j).wait_recv()
            to_z(l, j).wait_recv()
            to_corner(l, j).start()
            to_core(l, j, 1).start()
            to_core(l, j, 2).start()

    def stage_last(l):
        for j in hops:
            to_corner(l, j).wait_recv()
            to_core(l, j, 3).start()
        for j in hops:
            for kind in range(4):
                to_core(l, j, kind).wait_recv()
        to_sibling(l).wait_recv()
        own(l).wait()

    inner = up.shape[3]
    lanes = w.shape[4]
    width = z.shape[1]
    out_rows = w.shape[3] // 2

    def loader(l, i):
        return lambda: jnp.concatenate([w[l, i, k, :, :inner] for k in range(n_seq)], axis=0)

    def out_loader(l):
        def load():
            left = [w[l, 3, k, :out_rows, :] for k in range(n_seq)]
            right = [w[l, 3, k, out_rows:, : width - lanes] for k in range(n_seq)]
            return jnp.concatenate(left, axis=0), jnp.concatenate(right, axis=0)

        return load

    def exchange(values, sent, got, send, recv):
        batch, blocks, span = sent.shape[:3]
        for b in range(batch):
            for k in range(blocks):
                start = (b * blocks + k) * span
                sent[b, k] = values[start : start + span].astype(BF)
        copies = [
            remote(
                sent.at[:, seq_at(j)], got.at[:, s], send.at[j - 1], recv.at[j - 1],
                (d, seq_at(j)),
            )
            for j in range(1, n_seq)
        ]
        for copy in copies:
            copy.start()
        got[:, s] = sent[:, s]
        return copies

    def received(copies, got):
        for copy in copies:
            copy.wait_recv()
        return jnp.concatenate(
            [
                got[b, k].astype(F32)
                for b in range(got.shape[0])
                for k in range(got.shape[1])
            ],
            axis=0,
        )

    part_rows = wide.shape[3]
    block_parts = down.shape[2] * 2 // part_rows
    down_blocks = width // 128
    up_blocks = -(-inner // 128)
    used = (down_blocks + up_blocks) * block_parts
    all_sends = []

    def spot(p):
        return p // n_dp, p % n_dp

    def fan(count, source, dest, send, recv, target):
        copies = [
            remote(source(j), dest(j), send.at[j - 1], recv.at[j - 1], target(j))
            for j in range(1, count)
        ]
        for copy in copies:
            copy.start()
        all_sends.extend(copies)
        return copies

    def to_seq(j):
        return d, seq_at(j)

    def to_dp(j):
        return dp_at(j), s

    def landed(copies):
        for copy in copies:
            copy.wait_recv()

    def sum_first(l, grad_down, grad_up):
        fill = jnp.zeros((grad_up.shape[0], up_blocks * 128 - inner), F32)
        grad_up = jnp.concatenate([grad_up, fill], axis=1)
        for p in range(n_dp * n_seq):
            i, k = spot(p)
            if p >= used:
                wide[l, i, k] = jnp.zeros((part_rows, 128), BF)
                continue
            c, h = p // block_parts, p % block_parts
            values = grad_down if c < down_blocks else grad_up
            c = c if c < down_blocks else c - down_blocks
            rows = values[h * part_rows : (h + 1) * part_rows, c * 128 : (c + 1) * 128]
            wide[l, i, k] = rows.astype(BF)
        return fan(
            n_seq, lambda j: wide.at[l, seq_at(j)], lambda j: got_seq.at[l, j - 1],
            s1.at[l], r1.at[l], to_seq,
        )

    def sum_second(l, copies):
        landed(copies)
        total = wide[l, s].astype(F32)
        for j in range(1, n_seq):
            total = total + got_seq[l, j - 1].astype(F32)
        part[l] = total.astype(BF)
        return fan(
            n_dp, lambda j: part.at[l, dp_at(j)], lambda j: got_dp.at[l, j - 1],
            s2.at[l], r2.at[l], to_dp,
        )

    def sum_third(l, copies):
        landed(copies)
        total = part[l, d].astype(F32)
        for j in range(1, n_dp):
            total = total + got_dp[l, j - 1].astype(F32)
        full[l, s, d] = total.astype(BF)
        return fan(
            n_dp, lambda j: full.at[l, s, d], lambda j: full.at[l, s, d],
            s3.at[l], r3.at[l], to_dp,
        )

    def sum_fourth(l, copies):
        landed(copies)
        return fan(
            n_seq, lambda j: full.at[l, s], lambda j: full.at[l, s], s4.at[l], r4.at[l], to_seq
        )

    def sum_last(l, copies):
        landed(copies)
        for p in range(used):
            i, k = spot(p)
            c, h = p // block_parts, p % block_parts
            rows = pl.ds(h * part_rows, part_rows)
            values = full[l, i, k].astype(F32) * factor
            if c < down_blocks:
                all_down[l, rows, c * 128 : (c + 1) * 128] = values
            else:
                start = (c - down_blocks) * 128
                stop = min(start + 128, inner)
                all_up[l, rows, start:stop] = values[:, : stop - start]

    stage_first(0)
    stage_near(0)
    tokens = z.shape[0]
    first = Layer(z[...], mod, 0, down, up, 0, spatial_mask(tokens, positions))
    stage_pass(0)
    stage_first(1)
    stage_near(1)
    stage_corner(0)
    stage_pass(1)
    stage_last(0)
    weights_s = [loader(0, i) for i in range(3)]
    first.project(*weights_s)
    first.attend()
    hidden = first.output(out_loader(0))
    out_copies = exchange(hidden, sent_hidden, got_hidden, h_send, h_recv)
    stage_corner(1)
    by_position = received(out_copies, got_hidden)
    second = Layer(
        by_position, mod, 3, down, up, 1,
        temporal_mask(tokens, mod.shape[0], got_hidden.shape[2]),
    )
    stage_last(1)
    weights_t = [loader(1, i) for i in range(3)]
    second.project(*weights_t)
    second.attend()
    back, down_t, up_t = second.backward(
        upstream[...].astype(F32), *weights_t, out_loader(1)
    )
    back_copies = exchange(back, sent_back, got_back, b_send, b_recv)
    sum_t = sum_first(1, down_t, up_t)
    by_frame = received(back_copies, got_back)
    sum_t = sum_second(1, sum_t)
    result, down_s, up_s = first.backward(by_frame, *weights_s, out_loader(0))
    sum_s = sum_first(0, down_s, up_s)
    sum_t = sum_third(1, sum_t)
    grad[...] = result.astype(BF)
    sum_s = sum_second(0, sum_s)
    sum_t = sum_fourth(1, sum_t)
    sum_s = sum_third(0, sum_s)
    sum_s = sum_fourth(0, sum_s)
    sum_last(1, sum_t)
    sum_last(0, sum_s)
    for copy in out_copies + back_copies + all_sends:
        copy.wait_send()
    for l in range(2):
        to_sibling(l).wait_send()
        for j in hops:
            across(l, j).wait_send()
            to_y(l, j).wait_send()
            to_z(l, j).wait_send()
            to_corner(l, j).wait_send()
            for kind in range(4):
                to_core(l, j, kind).wait_send()


def stacked(w_in, w_out, lanes):
    left, right = w_out[:, :lanes], w_out[:, lanes:]
    right = jnp.pad(right, ((0, 0), (0, lanes - right.shape[1])))
    w_in = jnp.pad(w_in, ((0, 0), (0, 0), (0, lanes - w_in.shape[2])))
    return jnp.concatenate([w_in, jnp.concatenate([left, right], axis=0)[None]], axis=0)


def per_device(n_dp, n_seq, z, upstream, mod, in_s, out_s, in_t, out_t, down, up):
    batch, frames_here, positions, width = z.shape
    frames = frames_here * n_seq
    span = positions // n_seq
    inner, rank = up.shape[3], up.shape[2]
    tokens = batch * frames_here * positions
    factor = float(batch * n_dp * frames * positions) ** (-0.5)
    lanes = -(-inner // 128) * 128
    links = 2 * max(n_seq // 2 - 1, 1)
    shape = jax.ShapeDtypeStruct
    dma = pltpu.SemaphoreType.DMA
    buffer = pltpu.VMEM((batch, n_seq, span, width), BF)
    pair, hop, lane = dma((2,)), dma((2, links)), dma((n_seq - 1,))
    grads = [shape((2, 2 * rank, width), F32), shape((2, 2 * rank, inner), F32)]
    needed = 2 * rank * (width // 128 + -(-inner // 128))
    part_rows = 16
    while part_rows * n_dp * n_seq < needed:
        part_rows *= 2
    part = (part_rows, 128)
    seq_sem, dp_sem = dma((2, n_seq - 1)), dma((2, n_dp - 1))
    grad, all_down, all_up = pl.pallas_call(
        functools.partial(layers_kernel, n_dp, n_seq, positions, factor),
        out_shape=[shape((tokens, width), BF)] + grads,
        in_specs=[VMEM] * 5 + [ANY] * 2,
        out_specs=[VMEM] * 3,
        scratch_shapes=[pltpu.VMEM((2, 4, n_seq) + (in_s.shape[1], lanes), BF)]
        + [
            pltpu.VMEM((2,) + lead + part, BF)
            for lead in ((n_seq, n_dp), (n_seq - 1, n_dp), (n_dp,), (n_dp - 1,), (n_seq, n_dp))
        ]
        + [buffer] * 4
        + [pair] * 3
        + [hop] * 8
        + [dma((2, links, 4))] * 2
        + [lane] * 4
        + [seq_sem] * 2
        + [dp_sem] * 4
        + [seq_sem] * 2,
        compiler_params=pltpu.CompilerParams(
            collective_id=0, has_side_effects=True, vmem_limit_bytes=VMEM_BYTES
        ),
    )(
        z.reshape(tokens, width), upstream.reshape(tokens, width), mod, down, up,
        stacked(in_s, out_s, lanes), stacked(in_t, out_t, lanes),
    )
    return grad.reshape(z.shape), all_down.reshape(down.shape), all_up.reshape(up.shape)


def solution(mesh):
    placed = (
        P("dp", "seq", None, None),
        P("dp", None, "seq", None),
        P("dp", None, None),
        P(None, "seq", None),
        P("seq", None),
        P(None, "seq", None),
        P("seq", None),
        P(),
        P(),
    )
    return jax.shard_map(
        functools.partial(per_device, mesh.shape["dp"], mesh.shape["seq"]),
        mesh=mesh,
        in_specs=placed,
        out_specs=(P("dp", "seq", None, None), P(), P()),
        check_vma=False,
    )
```
